32 devices in a mesh: blk: 16 (over z, y, x), rep: 2 (over core).
Axes of the slice: x: 2, y: 2, z: 4, core: 2. Of those that a mesh axis runs over, the one named last changes fastest.
Arguments:
- points: float32 [64, 16384], P(None, 'blk'), may hold values from -1 to 1
- lengthscale: float32 [64], replicated, may hold values from 0.5 to 2
- noise: float32 [16384], P('blk'), may hold values from 0.5 to 2
- target: float32 [16, 16384], P(None, 'blk'), may hold values from -20 to 20
- pair_offset: int32 [16, 8], P('blk'), may hold values from 1 to 8, as said below
- pair_count: int32 [16], P('blk'), may hold values from 0 to 8
Outputs:
- solution: float32 [16, 16384], P(None, 'blk')
- residual: float32 [16, 16384], P(None, 'blk')
The draws below stay inside these ranges and needn't reach their ends.
Inputs may be any that keep to these rules, and one draw needn't show every extreme that they name: `pair_offset`: in row b the first pair_count[b] entries are distinct and b plus each of them is below 16; the other entries are unused.
All inputs are finite; a program needn't handle non-finite values.
Results may differ from the reference program's by a relative error of at most 0.0003.
Values may be sent and summed in bfloat16 or wider, within the bound.
A program may use at most 64 MiB of HBM per device.

```python
import math
import jax
import jax.numpy as jnp
from jax import lax

F = 64
B = 1024
C = 16
W = 8
ITERS = 2
NBLK = 16
NPTS = 16384


def shuffle_row(row_key):
    return jax.random.permutation(row_key, W).astype(jnp.int32)


def pair_tables(key):
    base_key = jax.random.fold_in(key, 11)
    keys = jax.random.split(base_key, 4)
    blocks = jnp.arange(NBLK, dtype=jnp.int32)
    room = jnp.minimum(W, NBLK - 1 - blocks)
    left_factor = jax.random.randint(keys[0], (NBLK,), 0, 5)
    right_factor = jax.random.randint(keys[1], (NBLK,), 0, 5)
    full_row = jax.random.randint(keys[2], (), 0, NBLK - W)
    counts = jnp.minimum(room, 1 + left_factor * right_factor // 2)
    counts = jnp.where(blocks == full_row, W, counts)
    shuffled = jax.vmap(shuffle_row)(jax.random.split(keys[3], NBLK)) + 1
    position = jnp.arange(W, dtype=jnp.int32)[None, :]
    ranking = jnp.where(shuffled <= room[:, None], 0, W) + position
    order = jnp.argsort(ranking, axis=1)
    offsets = jnp.take_along_axis(shuffled, order, axis=1)
    return (offsets.astype(jnp.int32), counts.astype(jnp.int32))


def draw_pair_offset(key, part):
    return pair_tables(key)[0]


def draw_pair_count(key, part):
    return pair_tables(key)[1]


def draw_points(key, part):
    keys = jax.random.split(jax.random.fold_in(key, 23), 4)
    along_blocks = jnp.arange(NPTS, dtype=jnp.float32) / B
    rate = jax.random.uniform(keys[0], (F, 1), jnp.float32, 0.04, 0.2)
    phase = jax.random.uniform(keys[1], (F, 1), jnp.float32, -3.14159, 3.14159)
    point_scale = jnp.exp(jax.random.uniform(keys[2], (1, NPTS), jnp.float32, -1.0, 1.0))
    rough_size = (0.035 / F) ** 0.5
    drift_size = (0.8 / F) ** 0.5
    rough = jnp.clip(jax.random.normal(keys[3], (F, NPTS), jnp.float32), -4.0, 4.0)
    drift = drift_size * jnp.sin(rate * along_blocks[None, :] + phase)
    return drift + rough_size * point_scale * rough


def draw_target(key, part):
    keys = jax.random.split(jax.random.fold_in(key, 31), 5)
    along = jnp.arange(NPTS, dtype=jnp.float32) / NPTS
    along_blocks = jnp.arange(NPTS, dtype=jnp.float32) / B
    rate = jax.random.uniform(keys[2], (C, 1), jnp.float32, 0.05, 0.3)
    phase = jax.random.uniform(keys[3], (C, 1), jnp.float32, -3.14159, 3.14159)
    base = jnp.clip(jax.random.normal(keys[0], (C, NPTS), jnp.float32), -5.0, 5.0)
    ramp = 1.0 + 2.0 * along
    level = jax.random.uniform(keys[4], (C, 1), jnp.float32, 0.5, 1.5)
    smooth = level + 0.8 * jnp.sin(rate * along_blocks[None, :] + phase)
    return base * ramp[None, :] + smooth


def level_of(rng, extent, cuts, least, top_value):
    loudness, own = 1.0, jax.random.fold_in(rng, 6)
    for axis_at, blocks in cuts:
        heights = jnp.exp(jax.random.uniform(jax.random.fold_in(own, axis_at), (blocks,), jnp.float32, least / len(cuts), top_value / len(cuts)))
        loudness = loudness * jnp.repeat(heights, extent[axis_at] // blocks).reshape([-1 if axis == axis_at else 1 for axis in range(len(extent))])
    return loudness


def setup_inputs(seed: int = 0) -> dict:
    key_list = jax.random.split(jax.random.key(seed), 7)
    return {
        "points": draw_points(jax.random.fold_in(key_list[6], 71), 0),
        "lengthscale": jnp.clip(jnp.exp(jax.random.uniform(key_list[1], (F,), jnp.float32, math.log(0.5), math.log(2.0))), 0.5, 2.0),
        "noise": jnp.clip(jnp.exp(math.log(2.0) - 1.3862944 * jax.random.uniform(key_list[2], (NPTS,), jnp.float32) ** level_of(key_list[2], (NPTS,), ((0, 16),), -0.2, 0.2)), 0.5, 2.0),
        "target": draw_target(jax.random.fold_in(key_list[6], 71), 0),
        "pair_offset": draw_pair_offset(jax.random.fold_in(key_list[6], 71), 0),
        "pair_count": draw_pair_count(jax.random.fold_in(key_list[6], 71), 0),
    }


exact = lax.Precision.HIGHEST

def kernel_tile(rows_z, cols_z):
    inner_prod = lax.dot_general(rows_z, cols_z, (((0,), (0,)), ((), ())), precision=exact, preferred_element_type=jnp.float32)
    square = lax.optimization_barrier(jnp.sum(rows_z * rows_z, axis=0))[:, None] + lax.optimization_barrier(jnp.sum(cols_z * cols_z, axis=0))[None, :] - 2.0 * inner_prod
    radius = jnp.sqrt(jnp.maximum(square, 0.0))
    margin = jnp.maximum(1.0 - radius, 0.0)
    margin_sq = margin * margin
    return 1.0 / B * margin_sq * margin_sq * (4.0 * radius + 1.0)

def apply_tile(vectors, kernel_low):
    return lax.dot_general(vectors, kernel_low, (((1,), (1,)), ((), ())), preferred_element_type=jnp.float32)

def reference(points, lengthscale, noise, target, pair_offset, pair_count):
    scaled = points / lengthscale[:, None]
    blocks = jnp.arange(NBLK, dtype=jnp.int32)

    def operate(direction):
        rounded = direction.astype(jnp.bfloat16)

        def per_block(state_now, block_id):
            product, degree = state_now
            own_start = (block_id * B).astype(jnp.int32)
            own_z = lax.dynamic_slice_in_dim(scaled, own_start, B, 1)
            own_v = lax.dynamic_slice_in_dim(rounded, own_start, B, 1)
            kernel = kernel_tile(own_z, own_z)
            own_prod = apply_tile(own_v, kernel.astype(jnp.bfloat16))
            own_deg = lax.optimization_barrier(jnp.sum(kernel, axis=1))
            for slot_id in range(W):
                is_live = slot_id < pair_count[block_id]
                partner = jnp.minimum(block_id + pair_offset[block_id, slot_id], NBLK - 1)
                partner_start = (partner * B).astype(jnp.int32)
                part_z = lax.dynamic_slice_in_dim(scaled, partner_start, B, 1)
                part_v = lax.dynamic_slice_in_dim(rounded, partner_start, B, 1)
                kernel = jnp.where(is_live, kernel_tile(own_z, part_z), 0.0)
                kernel_low = kernel.astype(jnp.bfloat16)
                own_prod = own_prod + apply_tile(part_v, kernel_low)
                own_deg = own_deg + lax.optimization_barrier(jnp.sum(kernel, axis=1))
                toward = jnp.dot(own_v, kernel_low, preferred_element_type=jnp.float32)
                product = lax.dynamic_update_slice_in_dim(product, lax.dynamic_slice_in_dim(product, partner_start, B, 1) + toward, partner_start, 1)
                degree = lax.dynamic_update_slice_in_dim(degree, lax.dynamic_slice_in_dim(degree, partner_start, B, 0) + lax.optimization_barrier(jnp.sum(kernel, axis=0)), partner_start, 0)
            product = lax.dynamic_update_slice_in_dim(product, lax.dynamic_slice_in_dim(product, own_start, B, 1) + own_prod, own_start, 1)
            degree = lax.dynamic_update_slice_in_dim(degree, lax.dynamic_slice_in_dim(degree, own_start, B, 0) + own_deg, own_start, 0)
            return ((product, degree), None)
        initial = (jnp.zeros(direction.shape, jnp.float32), jnp.zeros((NPTS,), jnp.float32))
        (product, degree), ignored = lax.scan(per_block, initial, blocks)
        return (noise + degree)[None, :] * direction + product
    solution = jnp.zeros_like(target)
    residual = target
    direction = target
    norm_now = lax.optimization_barrier(jnp.sum(residual * residual, axis=1))
    for iteration in range(ITERS):
        applied = operate(direction)
        step_size = norm_now / lax.optimization_barrier(jnp.sum(direction * applied, axis=1))
        solution = solution + step_size[:, None] * direction
        residual = residual - step_size[:, None] * applied
        if iteration + 1 < ITERS:
            norm_next = lax.optimization_barrier(jnp.sum(residual * residual, axis=1))
            direction = residual + (norm_next / norm_now)[:, None] * direction
            norm_now = norm_next
    return (solution, residual)
```

```python
import functools

import jax
import jax.numpy as jnp
from jax import lax
from jax.experimental import pallas as pl
from jax.experimental.pallas import tpu as pltpu
from jax.sharding import PartitionSpec as P

W = 8
SLOTS = W // 2
ROWS = 256
SUB = 16
DEPTH = 512
MESH = pl.DeviceIdType.MESH
f32 = jnp.float32
bf16 = jnp.bfloat16


def split3(value):
    hi = value.astype(bf16).astype(f32)
    rest = value - hi
    mid = rest.astype(bf16).astype(f32)
    return hi, mid, rest - mid


def lanes(value):
    total = value[:, 0:128]
    for at in range(128, value.shape[1], 128):
        total = total + value[:, at : at + 128]
    return total


def kernel(
    n, points, scale, noise, target, listed, sol, res,
    z, zp, left, right, sq, tiles, diag, rowacc, total, image, resid, low,
    vp1, vp2, out1, in1, out2, in2, half1, half2, mine, sums,
    zs, zr, v1s, v1r, v2s, v2r, r1s, r1r, r2s, r2r, hs, hr, ss, sr,
):
    blk = lax.axis_index("blk")
    core = lax.axis_index("rep")
    feats, size = points.shape
    cols = target.shape[0]
    half = size // 2

    def offset(k):
        return 1 + 2 * k + core

    def at(block):
        return {"blk": block, "rep": core}

    barrier = pltpu.get_barrier_semaphore()

    @pl.loop(0, n)
    def _(b):
        @pl.when(b != blk)
        def _():
            pl.semaphore_signal(barrier, inc=1, device_id=at(b), device_id_type=MESH)

    pl.semaphore_signal(
        barrier, inc=1, device_id={"blk": blk, "rep": 1 - core}, device_id_type=MESH
    )
    scaled = points[...] / scale[...]
    z[...] = scaled
    low[0] = target[...].astype(bf16)
    pl.semaphore_wait(barrier, n)

    def copy(src, dst, send, recv, block):
        return pltpu.make_async_remote_copy(
            src_ref=src, dst_ref=dst, send_sem=send, recv_sem=recv,
            device_id=at(block), device_id_type=MESH,
        )

    def z_copy(k):
        return copy(z, zp.at[k], zs.at[k], zr.at[k], blk - offset(k))

    def v1_copy(k):
        return copy(low.at[0], vp1.at[k], v1s.at[k], v1r.at[k], blk - offset(k))

    def v2_copy(k):
        return copy(low.at[1], vp2.at[k], v2s.at[k], v2r.at[k], blk - offset(k))

    def ret1_copy(k):
        return copy(out1.at[k], in1.at[k], r1s.at[k], r1r.at[k], blk + offset(k))

    def ret2_copy(k):
        return copy(out2.at[k], in2.at[k], r2s.at[k], r2r.at[k], blk + offset(k))

    def below(k):
        return blk - offset(k) >= 0

    def above(k):
        return blk + offset(k) < n

    for k in range(SLOTS):
        @pl.when(below(k))
        def _(k=k):
            z_copy(k).start()
            v1_copy(k).start()

    def norm_rows(value, first):
        n1, n2, n3 = split3(jnp.sum(value * value, axis=0, keepdims=True))
        i = lax.broadcasted_iota(jnp.int32, (16, size), 0)
        ones = jnp.where((i >= 3 - first) & (i < 6 - first), 1.0, 0.0)
        return jnp.where(
            i == first, n1, jnp.where(i == first + 1, n2, jnp.where(i == first + 2, n3, ones))
        )

    def fill_right(value):
        hi, mid, lo = split3(value)
        for j, part in enumerate((hi, mid, hi, mid, lo, hi)):
            right[j * feats : (j + 1) * feats, :] = part.astype(bf16)
        right[6 * feats : 6 * feats + 16, :] = norm_rows(value, 3).astype(bf16)

    right[6 * feats + 16 :, :] = jnp.zeros((DEPTH - 6 * feats - 16, size), bf16)
    hi, mid, lo = split3(-2.0 * scaled)
    hi2 = jnp.concatenate([hi, hi], axis=0)
    mid2 = jnp.concatenate([mid, mid], axis=0)
    hilo = jnp.concatenate([hi, lo], axis=0)
    tail = jnp.concatenate(
        [norm_rows(scaled, 0), jnp.zeros((112, size), f32)], axis=0
    )
    for j, part in enumerate((hi2, mid2, hilo, tail)):
        left[:, j * 128 : (j + 1) * 128] = part.T.astype(bf16)
    fill_right(scaled)

    def chunk(row, store, weight, with_rows, colacc):
        sq[...] = jnp.dot(
            left[pl.ds(row, ROWS), :], right[...], preferred_element_type=f32
        )
        for sub in range(0, ROWS, SUB):
            square = jnp.maximum(sq[sub : sub + SUB, :], 1e-24)
            radius = square * lax.rsqrt(square)
            margin = jnp.maximum(1.0 - radius, 0.0)
            margin = margin * margin
            value = margin * margin * (radius * (4.0 * weight) + weight)
            store(sub, value.astype(bf16))
            for g in range(0, SUB, 8):
                colacc = colacc + value[g : g + 8, :]
            if with_rows:
                rowacc[pl.ds(pl.multiple_of(row + sub, 8), SUB), :] += lanes(value)
        return colacc

    rowacc[...] = jnp.zeros_like(rowacc)
    inv = 1.0 / size

    def diag_chunk(j, colacc):
        def store(sub, value):
            diag[pl.ds(pl.multiple_of(j * ROWS + sub, 16), SUB), :] = value

        row = pl.multiple_of(core * half + j * ROWS, ROWS)
        return chunk(row, store, inv, False, colacc)

    colacc = lax.fori_loop(0, half // ROWS, diag_chunk, jnp.zeros((8, size), f32))
    own_cols = pl.ds(pl.multiple_of(core * half, 128), half)
    total[0:cols, :] = jnp.dot(low[0, :, own_cols], diag[...], preferred_element_type=f32)
    total[cols:, :] = jnp.zeros((8, size), f32)
    total[cols : cols + 1, :] = jnp.sum(colacc, axis=0, keepdims=True)

    def back(value, tile):
        return lax.dot_general(
            value, tile, (((1,), (1,)), ((), ())), preferred_element_type=f32
        )

    @pl.loop(0, SLOTS)
    def _(k):
        @pl.when(above(k))
        def _():
            z_copy(k).wait_recv()
            v1_copy(k).wait_recv()
            fill_right(zp[k])
            weight = listed[0, offset(k) - 1] * inv

            def step(j, colacc):
                def store(sub, value):
                    tiles[k, pl.ds(pl.multiple_of(j * ROWS + sub, 16), SUB), :] = value

                return chunk(pl.multiple_of(j * ROWS, ROWS), store, weight, True, colacc)

            colacc = lax.fori_loop(0, size // ROWS, step, jnp.zeros((8, size), f32))
            tile = tiles.at[k]
            out1[k, 0:cols, :] = jnp.dot(low[0], tile[...], preferred_element_type=f32)
            out1[k, cols:, :] = jnp.broadcast_to(
                jnp.sum(colacc, axis=0, keepdims=True), (8, size)
            )
            ret1_copy(k).start()
            total[0:cols, :] += back(vp1[k], tile[...])

    total[cols : cols + 1, :] += jnp.sum(rowacc[...].T, axis=0, keepdims=True)

    def collect(inbox, get, dst, send, recv):
        for k in range(SLOTS):
            @pl.when(below(k))
            def _(k=k):
                get(k).wait_recv()
                total[0 : inbox.shape[1], :] += inbox[k]

        src = total.at[pl.ds(0, inbox.shape[1])]
        swap = pltpu.make_async_remote_copy(
            src_ref=src, dst_ref=dst, send_sem=send, recv_sem=recv,
            device_id={"blk": blk, "rep": 1 - core}, device_id_type=MESH,
        )
        swap.start()
        swap.wait()

    def sum_start(which, values):
        for j, value in enumerate(values):
            mine[which, j * cols : (j + 1) * cols, :] = lanes(value)
        sums[which, pl.ds(blk, 1)] = mine[pl.ds(which, 1)]

        @pl.loop(0, n)
        def _(b):
            @pl.when(b != blk)
            def _():
                copy(mine.at[which], sums.at[which, blk], ss.at[which, b], sr.at[which, blk], b).start()

    def sum_end(which):
        @pl.loop(0, n)
        def _(b):
            @pl.when(b != blk)
            def _():
                one = copy(mine.at[which], sums.at[which, b], ss.at[which, b], sr.at[which, b], b)
                one.wait_recv()
                one.wait_send()

        return jnp.sum(jnp.sum(sums[which], axis=0), axis=1, keepdims=True)

    collect(in1, ret1_copy, half1, hs.at[0], hr.at[0])
    total[...] += half1[...]
    direction = target[...]
    diagonal = total[cols : cols + 1, :] + noise[...]
    image[...] = diagonal * direction + total[0:cols, :]
    sum_start(0, (direction * direction, direction * image[...]))
    both = sum_end(0)
    norm_now = both[0:cols]
    step1 = norm_now / both[cols : 2 * cols]
    residual = target[...] - step1 * image[...]
    resid[...] = residual
    low[1] = residual.astype(bf16)
    for k in range(SLOTS):
        @pl.when(below(k))
        def _(k=k):
            v2_copy(k).start()
    sum_start(1, (residual * residual, jnp.zeros_like(residual)))

    total[0:cols, :] = jnp.dot(low[1, :, own_cols], diag[...], preferred_element_type=f32)

    @pl.loop(0, SLOTS)
    def _(k):
        @pl.when(above(k))
        def _():
            tile = tiles.at[k]
            out2[k] = jnp.dot(low[1], tile[...], preferred_element_type=f32)
            ret2_copy(k).start()
            v2_copy(k).wait_recv()
            total[0:cols, :] += back(vp2[k], tile[...])

    norm_next = sum_end(1)[0:cols]
    collect(in2, ret2_copy, half2, hs.at[1], hr.at[1])
    beta = norm_next / norm_now
    direction = resid[...] + beta * target[...]
    image2 = (
        diagonal * resid[...] + (total[0:cols, :] + half2[...]) + beta * image[...]
    )
    dots = direction * image2
    sum_start(2, (dots, jnp.zeros_like(dots)))
    step2 = norm_next / sum_end(2)[0:cols]
    sol[...] = step1 * target[...] + step2 * direction
    res[...] = resid[...] - step2 * image2

    for k in range(SLOTS):
        @pl.when(below(k))
        def _(k=k):
            z_copy(k).wait_send()
            v1_copy(k).wait_send()
            v2_copy(k).wait_send()

        @pl.when(above(k))
        def _(k=k):
            ret1_copy(k).wait_send()
            ret2_copy(k).wait_send()


def body(n, points, lengthscale, noise, target, pair_offset, pair_count):
    feats, size = points.shape
    cols = target.shape[0]
    live = jnp.arange(W)[None, :] < pair_count[:, None]
    match = pair_offset[0][None, :] == jnp.arange(1, W + 1)[:, None]
    listed = jnp.any(match & live, axis=1).astype(f32)[None, :]
    vmem = pl.BlockSpec(memory_space=pltpu.VMEM)
    dma = pltpu.SemaphoreType.DMA
    V = pltpu.VMEM
    return pl.pallas_call(
        functools.partial(kernel, n),
        out_shape=[jax.ShapeDtypeStruct((cols, size), f32)] * 2,
        in_specs=[vmem, vmem, vmem, vmem, pl.BlockSpec(memory_space=pltpu.SMEM)],
        out_specs=[vmem, vmem],
        scratch_shapes=[
            V((feats, size), f32),
            V((SLOTS, feats, size), f32),
            V((size, DEPTH), bf16),
            V((DEPTH, size), bf16),
            V((ROWS, size), f32),
            V((SLOTS, size, size), bf16),
            V((size // 2, size), bf16),
            V((size, 128), f32),
            V((cols + 8, size), f32),
            V((cols, size), f32),
            V((cols, size), f32),
            V((2, cols, size), bf16),
            V((SLOTS, cols, size), bf16),
            V((SLOTS, cols, size), bf16),
            V((SLOTS, cols + 8, size), f32),
            V((SLOTS, cols + 8, size), f32),
            V((SLOTS, cols, size), f32),
            V((SLOTS, cols, size), f32),
            V((cols + 8, size), f32),
            V((cols, size), f32),
            V((3, 2 * cols, 128), f32),
            V((3, n, 2 * cols, 128), f32),
        ]
        + [dma((SLOTS,))] * 10
        + [dma((2,))] * 2
        + [dma((3, n))] * 2,
        compiler_params=pltpu.CompilerParams(
            collective_id=0, has_side_effects=True, vmem_limit_bytes=48 * 1024 * 1024
        ),
    )(points, lengthscale[:, None], noise[None, :], target, listed)


def solution(mesh):
    n = mesh.shape["blk"]
    placed = (P(None, "blk"), P(), P("blk"), P(None, "blk"), P("blk", None), P("blk"))
    return jax.shard_map(
        functools.partial(body, n),
        mesh=mesh,
        in_specs=placed,
        out_specs=(P(None, "blk"), P(None, "blk")),
        check_vma=False,
    )
```

```python
import functools

import jax
import jax.numpy as jnp
from jax import lax
from jax.experimental import pallas as pl
from jax.experimental.pallas import tpu as pltpu
from jax.sharding import PartitionSpec as P

W = 8
SLOTS = W // 2
ROWS = 256
SUB = 16
DEPTH = 512
MESH = pl.DeviceIdType.MESH
f32 = jnp.float32
bf16 = jnp.bfloat16


def split3(value):
    hi = value.astype(bf16).astype(f32)
    rest = value - hi
    mid = rest.astype(bf16).astype(f32)
    return hi, mid, rest - mid


def lanes(value):
    total = value[:, 0:128]
    for at in range(128, value.shape[1], 128):
        total = total + value[:, at : at + 128]
    return total


def kernel(
    n, points, scale, noise, target, listed, sol, res,
    z, zp, left, right, sq, tiles, diag, rowacc, total, image, resid, low,
    vp1, vp2, out1, in1, out2, in2, half1, half2, mine, sums,
    outd, ind, zs, zr, ds, dr, v1s, v1r, v2s, v2r, r1s, r1r, r2s, r2r, hs, hr, ss, sr,
):
    blk = lax.axis_index("blk")
    core = lax.axis_index("rep")
    feats, size = points.shape
    cols = target.shape[0]
    half = size // 2

    def offset(k):
        return 1 + 2 * k + core

    def at(block):
        return {"blk": block, "rep": core}

    first = lax.div(blk, 4) * 4

    def mate(m):
        return first + lax.rem(blk - first + m, 4)

    barrier = pltpu.get_barrier_semaphore()

    @pl.loop(0, n)
    def _(b):
        @pl.when(b != blk)
        def _():
            pl.semaphore_signal(barrier, inc=1, device_id=at(b), device_id_type=MESH)

    for m in range(4):
        pl.semaphore_signal(
            barrier, inc=1, device_id={"blk": mate(m), "rep": 1 - core}, device_id_type=MESH
        )
    scaled = points[...] / scale[...]
    z[...] = scaled
    low[0] = target[...].astype(bf16)
    pl.semaphore_wait(barrier, n + 3)

    def copy(src, dst, send, recv, block):
        return pltpu.make_async_remote_copy(
            src_ref=src, dst_ref=dst, send_sem=send, recv_sem=recv,
            device_id=at(block), device_id_type=MESH,
        )

    def z_send(src, shift, block, sem):
        slot, owner = lax.div(shift - 1, 2), lax.rem(shift - 1, 2)
        return pltpu.make_async_remote_copy(
            src_ref=src, dst_ref=zp.at[slot], send_sem=zs.at[sem], recv_sem=zr.at[slot],
            device_id={"blk": block, "rep": owner}, device_id_type=MESH,
        )

    def z_wait(k):
        copy(z, zp.at[k], zs.at[0], zr.at[k], blk).wait_recv()

    def own_sends(act):
        for m in (1, 2, 3):
            @pl.when((core == 0) & (mate(m) < blk))
            def _(m=m):
                act(z_send(z, blk - mate(m), mate(m), m - 1))

        @pl.when((core == 1) & (blk >= 4))
        def _():
            act(z_send(z, 4, blk - 4, 0))

    def relay_near(act):
        @pl.when(blk >= 4)
        def _():
            act(z_send(zp.at[1], 8, blk - 4, 1))

        for m in (1, 2, 3):
            act(z_send(zp.at[1], blk + 4 - mate(m), mate(m), 1 + m))

    def relay_far(act):
        for m in (1, 2, 3):
            @pl.when(mate(m) > blk)
            def _(m=m):
                act(z_send(zp.at[3], blk + 8 - mate(m), mate(m), 4 + m))

    def deg_copy(k):
        return copy(outd.at[k], ind.at[k], ds.at[k], dr.at[k], blk + offset(k))

    def v1_copy(k):
        return copy(low.at[0], vp1.at[k], v1s.at[k], v1r.at[k], blk - offset(k))

    def v2_copy(k):
        return copy(low.at[1], vp2.at[k], v2s.at[k], v2r.at[k], blk - offset(k))

    def ret1_copy(k):
        return copy(out1.at[k], in1.at[k], r1s.at[k], r1r.at[k], blk + offset(k))

    def ret2_copy(k):
        return copy(out2.at[k], in2.at[k], r2s.at[k], r2r.at[k], blk + offset(k))

    def below(k):
        return blk - offset(k) >= 0

    def above(k):
        return blk + offset(k) < n

    own_sends(lambda one: one.start())

    for k in range(SLOTS):
        @pl.when(below(k))
        def _(k=k):
            v1_copy(k).start()

    def norm_rows(value, first):
        n1, n2, n3 = split3(jnp.sum(value * value, axis=0, keepdims=True))
        i = lax.broadcasted_iota(jnp.int32, (16, size), 0)
        ones = jnp.where((i >= 3 - first) & (i < 6 - first), 1.0, 0.0)
        return jnp.where(
            i == first, n1, jnp.where(i == first + 1, n2, jnp.where(i == first + 2, n3, ones))
        )

    def fill_right(value):
        hi, mid, lo = split3(value)
        for j, part in enumerate((hi, mid, hi, mid, lo, hi)):
            right[j * feats : (j + 1) * feats, :] = part.astype(bf16)
        right[6 * feats : 6 * feats + 16, :] = norm_rows(value, 3).astype(bf16)

    right[6 * feats + 16 :, :] = jnp.zeros((DEPTH - 6 * feats - 16, size), bf16)
    hi, mid, lo = split3(-2.0 * scaled)
    hi2 = jnp.concatenate([hi, hi], axis=0)
    mid2 = jnp.concatenate([mid, mid], axis=0)
    hilo = jnp.concatenate([hi, lo], axis=0)
    tail = jnp.concatenate(
        [norm_rows(scaled, 0), jnp.zeros((112, size), f32)], axis=0
    )
    for j, part in enumerate((hi2, mid2, hilo, tail)):
        left[:, j * 128 : (j + 1) * 128] = part.T.astype(bf16)
    fill_right(scaled)

    def chunk(row, store, weight, with_rows, colacc):
        sq[...] = jnp.dot(
            left[pl.ds(row, ROWS), :], right[...], preferred_element_type=f32
        )
        for sub in range(0, ROWS, SUB):
            square = jnp.maximum(sq[sub : sub + SUB, :], 1e-24)
            radius = square * lax.rsqrt(square)
            margin = jnp.maximum(1.0 - radius, 0.0)
            margin = margin * margin
            value = margin * margin * (radius * (4.0 * weight) + weight)
            store(sub, value.astype(bf16))
            for g in range(0, SUB, 8):
                colacc = colacc + value[g : g + 8, :]
            if with_rows:
                rowacc[pl.ds(pl.multiple_of(row + sub, 8), SUB), :] += lanes(value)
        return colacc

    rowacc[...] = jnp.zeros_like(rowacc)
    inv = 1.0 / size

    def diag_chunk(j, colacc):
        def store(sub, value):
            diag[pl.ds(pl.multiple_of(j * ROWS + sub, 16), SUB), :] = value

        row = pl.multiple_of(core * half + j * ROWS, ROWS)
        return chunk(row, store, inv, False, colacc)

    colacc = lax.fori_loop(0, half // ROWS, diag_chunk, jnp.zeros((8, size), f32))
    own_cols = pl.ds(pl.multiple_of(core * half, 128), half)
    total[0:cols, :] = jnp.dot(low[0, :, own_cols], diag[...], preferred_element_type=f32)
    total[cols:, :] = jnp.zeros((8, size), f32)
    total[cols : cols + 1, :] = jnp.sum(colacc, axis=0, keepdims=True)

    def back(value, tile):
        return lax.dot_general(
            value, tile, (((1,), (1,)), ((), ())), preferred_element_type=f32
        )

    @pl.when((core == 1) & (blk + 4 < n))
    def _():
        z_wait(1)
        relay_near(lambda one: one.start())

    @pl.when((core == 1) & (blk + 8 < n))
    def _():
        z_wait(3)
        relay_far(lambda one: one.start())

    @pl.loop(0, SLOTS)
    def _(step_k):
        k = lax.rem(step_k + core, SLOTS)

        @pl.when(above(k))
        def _():
            @pl.when((core == 0) | (lax.rem(k, 2) == 0))
            def _():
                z_wait(k)

            v1_copy(k).wait_recv()
            fill_right(zp[k])
            weight = listed[0, offset(k) - 1] * inv

            def step(j, colacc):
                def store(sub, value):
                    tiles[k, pl.ds(pl.multiple_of(j * ROWS + sub, 16), SUB), :] = value

                return chunk(pl.multiple_of(j * ROWS, ROWS), store, weight, True, colacc)

            colacc = lax.fori_loop(0, size // ROWS, step, jnp.zeros((8, size), f32))
            tile = tiles.at[k]
            outd[k] = jnp.sum(colacc, axis=0, keepdims=True)
            deg_copy(k).start()
            out1[k] = jnp.dot(low[0], tile[...], preferred_element_type=f32)
            ret1_copy(k).start()
            total[0:cols, :] += back(vp1[k], tile[...])

    total[cols : cols + 1, :] += jnp.sum(rowacc[...].T, axis=0, keepdims=True)

    def collect(inbox, get, dst, send, recv):
        for k in range(SLOTS):
            @pl.when(below(k))
            def _(k=k):
                get(k).wait_recv()
                total[0:cols, :] += inbox[k]

        src = total.at[pl.ds(0, dst.shape[0])]
        swap = pltpu.make_async_remote_copy(
            src_ref=src, dst_ref=dst, send_sem=send, recv_sem=recv,
            device_id={"blk": blk, "rep": 1 - core}, device_id_type=MESH,
        )
        swap.start()
        swap.wait()

    def spot(j):
        row = lax.broadcasted_iota(jnp.int32, (cols, 128), 0)
        return lax.broadcasted_iota(jnp.int32, (cols, 128), 1) == row + j * cols

    def sum_start(which, values):
        mine[which] = sum(
            jnp.sum(
                jnp.where(spot(j), jnp.sum(value, axis=1, keepdims=True), 0.0),
                axis=0, keepdims=True,
            )
            for j, value in enumerate(values)
        )
        sums[which, pl.ds(blk, 1)] = mine[pl.ds(which, 1)]

        @pl.loop(0, n)
        def _(b):
            @pl.when(b != blk)
            def _():
                copy(mine.at[which], sums.at[which, blk], ss.at[which, b], sr.at[which, blk], b).start()

    def sum_end(which, count):
        @pl.loop(0, n)
        def _(b):
            @pl.when(b != blk)
            def _():
                one = copy(mine.at[which], sums.at[which, b], ss.at[which, b], sr.at[which, b], b)
                one.wait_recv()
                one.wait_send()

        row = jnp.sum(sums[which], axis=0)
        return [
            jnp.sum(jnp.where(spot(j), row, 0.0), axis=1, keepdims=True) for j in range(count)
        ]

    for k in range(SLOTS):
        @pl.when(below(k))
        def _(k=k):
            deg_copy(k).wait_recv()
            total[cols : cols + 1, :] += ind[k]

    collect(in1, ret1_copy, half1, hs.at[0], hr.at[0])
    total[...] += half1[...]
    direction = target[...]
    diagonal = total[cols : cols + 1, :] + noise[...]
    image[...] = diagonal * direction + total[0:cols, :]
    sum_start(0, (direction * direction, direction * image[...]))
    norm_now, curve = sum_end(0, 2)
    step1 = norm_now / curve
    residual = target[...] - step1 * image[...]
    resid[...] = residual
    low[1] = residual.astype(bf16)
    for k in range(SLOTS):
        @pl.when(below(k))
        def _(k=k):
            v2_copy(k).start()
    sum_start(1, (residual * residual,))

    total[0:cols, :] = jnp.dot(low[1, :, own_cols], diag[...], preferred_element_type=f32)

    @pl.loop(0, SLOTS)
    def _(k):
        @pl.when(above(k))
        def _():
            tile = tiles.at[k]
            out2[k] = jnp.dot(low[1], tile[...], preferred_element_type=f32)
            ret2_copy(k).start()
            v2_copy(k).wait_recv()
            total[0:cols, :] += back(vp2[k], tile[...])

    norm_next = sum_end(1, 1)[0]
    collect(in2, ret2_copy, half2, hs.at[1], hr.at[1])
    beta = norm_next / norm_now
    direction = resid[...] + beta * target[...]
    image2 = (
        diagonal * resid[...] + (total[0:cols, :] + half2[...]) + beta * image[...]
    )
    sum_start(2, (direction * image2,))
    step2 = norm_next / sum_end(2, 1)[0]
    sol[...] = step1 * target[...] + step2 * direction
    res[...] = resid[...] - step2 * image2

    own_sends(lambda one: one.wait_send())

    @pl.when((core == 1) & (blk + 4 < n))
    def _():
        relay_near(lambda one: one.wait_send())

    @pl.when((core == 1) & (blk + 8 < n))
    def _():
        relay_far(lambda one: one.wait_send())

    for k in range(SLOTS):
        @pl.when(below(k))
        def _(k=k):
            v1_copy(k).wait_send()
            v2_copy(k).wait_send()

        @pl.when(above(k))
        def _(k=k):
            ret1_copy(k).wait_send()
            deg_copy(k).wait_send()
            ret2_copy(k).wait_send()


def body(n, points, lengthscale, noise, target, pair_offset, pair_count):
    feats, size = points.shape
    cols = target.shape[0]
    live = jnp.arange(W)[None, :] < pair_count[:, None]
    match = pair_offset[0][None, :] == jnp.arange(1, W + 1)[:, None]
    listed = jnp.any(match & live, axis=1).astype(f32)[None, :]
    vmem = pl.BlockSpec(memory_space=pltpu.VMEM)
    dma = pltpu.SemaphoreType.DMA
    V = pltpu.VMEM
    return pl.pallas_call(
        functools.partial(kernel, n),
        out_shape=[jax.ShapeDtypeStruct((cols, size), f32)] * 2,
        in_specs=[vmem, vmem, vmem, vmem, pl.BlockSpec(memory_space=pltpu.SMEM)],
        out_specs=[vmem, vmem],
        scratch_shapes=[
            V((feats, size), f32),
            V((SLOTS, feats, size), f32),
            V((size, DEPTH), bf16),
            V((DEPTH, size), bf16),
            V((ROWS, size), f32),
            V((SLOTS, size, size), bf16),
            V((size // 2, size), bf16),
            V((size, 128), f32),
            V((cols + 8, size), f32),
            V((cols, size), f32),
            V((cols, size), f32),
            V((2, cols, size), bf16),
            V((SLOTS, cols, size), bf16),
            V((SLOTS, cols, size), bf16),
            V((SLOTS, cols, size), f32),
            V((SLOTS, cols, size), f32),
            V((SLOTS, cols, size), f32),
            V((SLOTS, cols, size), f32),
            V((cols + 8, size), f32),
            V((cols, size), f32),
            V((3, 1, 128), f32),
            V((3, n, 1, 128), f32),
            V((SLOTS, 1, size), f32),
            V((SLOTS, 1, size), f32),
        ]
        + [dma((W,)), dma((SLOTS,))]
        + [dma((SLOTS,))] * 10
        + [dma((2,))] * 2
        + [dma((3, n))] * 2,
        compiler_params=pltpu.CompilerParams(
            collective_id=0, has_side_effects=True, vmem_limit_bytes=48 * 1024 * 1024
        ),
    )(points, lengthscale[:, None], noise[None, :], target, listed)


def solution(mesh):
    n = mesh.shape["blk"]
    placed = (P(None, "blk"), P(), P("blk"), P(None, "blk"), P("blk", None), P("blk"))
    return jax.shard_map(
        functools.partial(body, n),
        mesh=mesh,
        in_specs=placed,
        out_specs=(P(None, "blk"), P(None, "blk")),
        check_vma=False,
    )
```

```python
import functools

import jax
import jax.numpy as jnp
from jax import lax
from jax.experimental import pallas as pl
from jax.experimental.pallas import tpu as pltpu
from jax.sharding import PartitionSpec as P

W = 8
SLOTS = W // 2
ROWS = 256
SUB = 16
DEPTH = 512
MESH = pl.DeviceIdType.MESH
f32 = jnp.float32
bf16 = jnp.bfloat16


def split3(value):
    hi = value.astype(bf16).astype(f32)
    rest = value - hi
    mid = rest.astype(bf16).astype(f32)
    return hi, mid, rest - mid


def lanes(value):
    total = value[:, 0:128]
    for at in range(128, value.shape[1], 128):
        total = total + value[:, at : at + 128]
    return total


def kernel(
    n, points, scale, noise, target, listed, sol, res,
    z, zp, left, right, sq, tiles, diag, rowacc, total, image, resid, low,
    vp1, vp2, out1, in1, out2, in2, half1, half2, mine, sums,
    acc, outd, ind, zs, zr, ds, dr, v1s, v1r, v2s, v2r, r1s, r1r, r2s, r2r, hs, hr, ss, sr,
):
    blk = lax.axis_index("blk")
    core = lax.axis_index("rep")
    feats, size = points.shape
    cols = target.shape[0]
    half = size // 2

    def offset(k):
        return 1 + 2 * k + core

    def at(block):
        return {"blk": block, "rep": core}

    first = lax.div(blk, 4) * 4

    def mate(m):
        return first + lax.rem(blk - first + m, 4)

    barrier = pltpu.get_barrier_semaphore()

    @pl.loop(0, n)
    def _(b):
        @pl.when(b != blk)
        def _():
            pl.semaphore_signal(barrier, inc=1, device_id=at(b), device_id_type=MESH)

    for m in range(4):
        pl.semaphore_signal(
            barrier, inc=1, device_id={"blk": mate(m), "rep": 1 - core}, device_id_type=MESH
        )
    scaled = points[...] / scale[...]
    z[...] = scaled
    low[0] = target[...].astype(bf16)
    pl.semaphore_wait(barrier, n + 3)

    def copy(src, dst, send, recv, block):
        return pltpu.make_async_remote_copy(
            src_ref=src, dst_ref=dst, send_sem=send, recv_sem=recv,
            device_id=at(block), device_id_type=MESH,
        )

    def z_send(src, shift, block, sem):
        slot, owner = lax.div(shift - 1, 2), lax.rem(shift - 1, 2)
        return pltpu.make_async_remote_copy(
            src_ref=src, dst_ref=zp.at[slot], send_sem=zs.at[sem], recv_sem=zr.at[slot],
            device_id={"blk": block, "rep": owner}, device_id_type=MESH,
        )

    def z_wait(k):
        copy(z, zp.at[k], zs.at[0], zr.at[k], blk).wait_recv()

    def own_sends(act):
        for m in (1, 2, 3):
            @pl.when((core == 0) & (mate(m) < blk))
            def _(m=m):
                act(z_send(z, blk - mate(m), mate(m), m - 1))

        @pl.when((core == 1) & (blk >= 4))
        def _():
            act(z_send(z, 4, blk - 4, 0))

    def relay_near(act):
        @pl.when(blk >= 4)
        def _():
            act(z_send(zp.at[1], 8, blk - 4, 1))

        for m in (1, 2, 3):
            act(z_send(zp.at[1], blk + 4 - mate(m), mate(m), 1 + m))

    def relay_far(act):
        for m in (1, 2, 3):
            @pl.when(mate(m) > blk)
            def _(m=m):
                act(z_send(zp.at[3], blk + 8 - mate(m), mate(m), 4 + m))

    def deg_copy(k):
        return copy(outd.at[k], ind.at[k], ds.at[k], dr.at[k], blk + offset(k))

    def v1_copy(k):
        return copy(low.at[0], vp1.at[k], v1s.at[k], v1r.at[k], blk - offset(k))

    def v2_copy(k):
        return copy(low.at[1], vp2.at[k], v2s.at[k], v2r.at[k], blk - offset(k))

    def ret1_copy(k):
        return copy(out1.at[k], in1.at[k], r1s.at[k], r1r.at[k], blk + offset(k))

    def ret2_copy(k):
        return copy(out2.at[k], in2.at[k], r2s.at[k], r2r.at[k], blk + offset(k))

    def below(k):
        return blk - offset(k) >= 0

    def above(k):
        return blk + offset(k) < n

    own_sends(lambda one: one.start())

    for k in range(SLOTS):
        @pl.when(below(k))
        def _(k=k):
            v1_copy(k).start()

    def norm_rows(value, first):
        n1, n2, n3 = split3(jnp.sum(value * value, axis=0, keepdims=True))
        i = lax.broadcasted_iota(jnp.int32, (16, size), 0)
        ones = jnp.where((i >= 3 - first) & (i < 6 - first), 1.0, 0.0)
        return jnp.where(
            i == first, n1, jnp.where(i == first + 1, n2, jnp.where(i == first + 2, n3, ones))
        )

    def fill_right(value):
        hi, mid, lo = split3(value)
        for j, part in enumerate((hi, mid, hi, mid, lo, hi)):
            right[j * feats : (j + 1) * feats, :] = part.astype(bf16)
        right[6 * feats : 6 * feats + 16, :] = norm_rows(value, 3).astype(bf16)

    right[6 * feats + 16 :, :] = jnp.zeros((DEPTH - 6 * feats - 16, size), bf16)
    hi, mid, lo = split3(-2.0 * scaled)
    hi2 = jnp.concatenate([hi, hi], axis=0)
    mid2 = jnp.concatenate([mid, mid], axis=0)
    hilo = jnp.concatenate([hi, lo], axis=0)
    tail = jnp.concatenate(
        [norm_rows(scaled, 0), jnp.zeros((112, size), f32)], axis=0
    )
    for j, part in enumerate((hi2, mid2, hilo, tail)):
        left[:, j * 128 : (j + 1) * 128] = part.T.astype(bf16)
    fill_right(scaled)

    def chunk(row, store, weight, with_rows, colacc):
        sq[...] = jnp.dot(
            left[pl.ds(row, ROWS), :], right[...], preferred_element_type=f32
        )
        for sub in range(0, ROWS, SUB):
            square = jnp.maximum(sq[sub : sub + SUB, :], 1e-24)
            radius = square * lax.rsqrt(square)
            margin = jnp.maximum(1.0 - radius, 0.0)
            margin = margin * margin
            value = margin * margin * (radius * (4.0 * weight) + weight)
            store(sub, value.astype(bf16))
            for g in range(0, SUB, 8):
                colacc = colacc + value[g : g + 8, :]
            if with_rows:
                rowacc[pl.ds(pl.multiple_of(row + sub, 8), SUB), :] += lanes(value)
        return colacc

    rowacc[...] = jnp.zeros_like(rowacc)
    inv = 1.0 / size

    def diag_chunk(j, colacc):
        def store(sub, value):
            diag[pl.ds(pl.multiple_of(j * ROWS + sub, 16), SUB), :] = value

        row = pl.multiple_of(core * half + j * ROWS, ROWS)
        return chunk(row, store, inv, False, colacc)

    colacc = lax.fori_loop(0, half // ROWS, diag_chunk, jnp.zeros((8, size), f32))
    own_cols = pl.ds(pl.multiple_of(core * half, 128), half)
    total[0:cols, :] = jnp.dot(low[0, :, own_cols], diag[...], preferred_element_type=f32)
    total[cols:, :] = jnp.zeros((8, size), f32)
    total[cols : cols + 1, :] = jnp.sum(colacc, axis=0, keepdims=True)

    acc[...] = jnp.zeros_like(acc)

    def back(value, tile):
        wide = jnp.concatenate(
            [value.astype(f32), jnp.zeros((128 - cols, size), f32)], axis=0
        )
        acc[...] += jnp.dot(tile, wide.T.astype(bf16), preferred_element_type=f32)

    @pl.when((core == 1) & (blk + 4 < n))
    def _():
        z_wait(1)
        relay_near(lambda one: one.start())

    @pl.when((core == 1) & (blk + 8 < n))
    def _():
        z_wait(3)
        relay_far(lambda one: one.start())

    @pl.loop(0, SLOTS)
    def _(step_k):
        k = lax.rem(step_k + core, SLOTS)

        @pl.when(above(k))
        def _():
            @pl.when((core == 0) | (lax.rem(k, 2) == 0))
            def _():
                z_wait(k)

            v1_copy(k).wait_recv()
            fill_right(zp[k])
            weight = listed[0, offset(k) - 1] * inv

            def step(j, colacc):
                def store(sub, value):
                    tiles[k, pl.ds(pl.multiple_of(j * ROWS + sub, 16), SUB), :] = value

                return chunk(pl.multiple_of(j * ROWS, ROWS), store, weight, True, colacc)

            colacc = lax.fori_loop(0, size // ROWS, step, jnp.zeros((8, size), f32))
            tile = tiles.at[k]
            outd[k] = jnp.sum(colacc, axis=0, keepdims=True)
            deg_copy(k).start()
            out1[k] = jnp.dot(low[0], tile[...], preferred_element_type=f32)
            ret1_copy(k).start()
            back(vp1[k], tile[...])

    total[0:cols, :] += acc[...].T[0:cols, :]
    acc[...] = jnp.zeros_like(acc)
    total[cols : cols + 1, :] += jnp.sum(rowacc[...].T, axis=0, keepdims=True)

    def collect(inbox, get, dst, send, recv):
        for k in range(SLOTS):
            @pl.when(below(k))
            def _(k=k):
                get(k).wait_recv()
                total[0:cols, :] += inbox[k]

        src = total.at[pl.ds(0, dst.shape[0])]
        swap = pltpu.make_async_remote_copy(
            src_ref=src, dst_ref=dst, send_sem=send, recv_sem=recv,
            device_id={"blk": blk, "rep": 1 - core}, device_id_type=MESH,
        )
        swap.start()
        swap.wait()

    def spot(j):
        row = lax.broadcasted_iota(jnp.int32, (cols, 128), 0)
        return lax.broadcasted_iota(jnp.int32, (cols, 128), 1) == row + j * cols

    def sum_start(which, values):
        mine[which] = sum(
            jnp.sum(
                jnp.where(spot(j), jnp.sum(value, axis=1, keepdims=True), 0.0),
                axis=0, keepdims=True,
            )
            for j, value in enumerate(values)
        )
        sums[which, pl.ds(blk, 1)] = mine[pl.ds(which, 1)]

        @pl.loop(0, n)
        def _(b):
            @pl.when(b != blk)
            def _():
                copy(mine.at[which], sums.at[which, blk], ss.at[which, b], sr.at[which, blk], b).start()

    def sum_end(which, count):
        @pl.loop(0, n)
        def _(b):
            @pl.when(b != blk)
            def _():
                one = copy(mine.at[which], sums.at[which, b], ss.at[which, b], sr.at[which, b], b)
                one.wait_recv()
                one.wait_send()

        row = jnp.sum(sums[which], axis=0)
        return [
            jnp.sum(jnp.where(spot(j), row, 0.0), axis=1, keepdims=True) for j in range(count)
        ]

    for k in range(SLOTS):
        @pl.when(below(k))
        def _(k=k):
            deg_copy(k).wait_recv()
            total[cols : cols + 1, :] += ind[k]

    collect(in1, ret1_copy, half1, hs.at[0], hr.at[0])
    total[...] += half1[...]
    direction = target[...]
    diagonal = total[cols : cols + 1, :] + noise[...]
    image[...] = diagonal * direction + total[0:cols, :]
    sum_start(0, (direction * direction, direction * image[...]))
    norm_now, curve = sum_end(0, 2)
    step1 = norm_now / curve
    residual = target[...] - step1 * image[...]
    resid[...] = residual
    low[1] = residual.astype(bf16)
    for k in range(SLOTS):
        @pl.when(below(k))
        def _(k=k):
            v2_copy(k).start()
    sum_start(1, (residual * residual,))

    total[0:cols, :] = jnp.dot(low[1, :, own_cols], diag[...], preferred_element_type=f32)

    @pl.loop(0, SLOTS)
    def _(k):
        @pl.when(above(k))
        def _():
            out2[k] = jnp.dot(low[1], tiles[k], preferred_element_type=f32)
            ret2_copy(k).start()

    @pl.loop(0, SLOTS)
    def _(k):
        @pl.when(above(k))
        def _():
            v2_copy(k).wait_recv()
            back(vp2[k], tiles[k])

    total[0:cols, :] += acc[...].T[0:cols, :]

    norm_next = sum_end(1, 1)[0]
    collect(in2, ret2_copy, half2, hs.at[1], hr.at[1])
    beta = norm_next / norm_now
    direction = resid[...] + beta * target[...]
    image2 = (
        diagonal * resid[...] + (total[0:cols, :] + half2[...]) + beta * image[...]
    )
    sum_start(2, (direction * image2,))
    step2 = norm_next / sum_end(2, 1)[0]
    sol[...] = step1 * target[...] + step2 * direction
    res[...] = resid[...] - step2 * image2

    own_sends(lambda one: one.wait_send())

    @pl.when((core == 1) & (blk + 4 < n))
    def _():
        relay_near(lambda one: one.wait_send())

    @pl.when((core == 1) & (blk + 8 < n))
    def _():
        relay_far(lambda one: one.wait_send())

    for k in range(SLOTS):
        @pl.when(below(k))
        def _(k=k):
            v1_copy(k).wait_send()
            v2_copy(k).wait_send()

        @pl.when(above(k))
        def _(k=k):
            ret1_copy(k).wait_send()
            deg_copy(k).wait_send()
            ret2_copy(k).wait_send()


def body(n, points, lengthscale, noise, target, pair_offset, pair_count):
    feats, size = points.shape
    cols = target.shape[0]
    live = jnp.arange(W)[None, :] < pair_count[:, None]
    match = pair_offset[0][None, :] == jnp.arange(1, W + 1)[:, None]
    listed = jnp.any(match & live, axis=1).astype(f32)[None, :]
    vmem = pl.BlockSpec(memory_space=pltpu.VMEM)
    dma = pltpu.SemaphoreType.DMA
    V = pltpu.VMEM
    return pl.pallas_call(
        functools.partial(kernel, n),
        out_shape=[jax.ShapeDtypeStruct((cols, size), f32)] * 2,
        in_specs=[vmem, vmem, vmem, vmem, pl.BlockSpec(memory_space=pltpu.SMEM)],
        out_specs=[vmem, vmem],
        scratch_shapes=[
            V((feats, size), f32),
            V((SLOTS, feats, size), f32),
            V((size, DEPTH), bf16),
            V((DEPTH, size), bf16),
            V((ROWS, size), f32),
            V((SLOTS, size, size), bf16),
            V((size // 2, size), bf16),
            V((size, 128), f32),
            V((cols + 8, size), f32),
            V((cols, size), f32),
            V((cols, size), f32),
            V((2, cols, size), bf16),
            V((SLOTS, cols, size), bf16),
            V((SLOTS, cols, size), bf16),
            V((SLOTS, cols, size), f32),
            V((SLOTS, cols, size), f32),
            V((SLOTS, cols, size), f32),
            V((SLOTS, cols, size), f32),
            V((cols + 8, size), f32),
            V((cols, size), f32),
            V((3, 1, 128), f32),
            V((3, n, 1, 128), f32),
            V((size, 128), f32),
            V((SLOTS, 1, size), f32),
            V((SLOTS, 1, size), f32),
        ]
        + [dma((W,)), dma((SLOTS,))]
        + [dma((SLOTS,))] * 10
        + [dma((2,))] * 2
        + [dma((3, n))] * 2,
        compiler_params=pltpu.CompilerParams(
            collective_id=0, has_side_effects=True, vmem_limit_bytes=48 * 1024 * 1024
        ),
    )(points, lengthscale[:, None], noise[None, :], target, listed)


def solution(mesh):
    n = mesh.shape["blk"]
    placed = (P(None, "blk"), P(), P("blk"), P(None, "blk"), P("blk", None), P("blk"))
    return jax.shard_map(
        functools.partial(body, n),
        mesh=mesh,
        in_specs=placed,
        out_specs=(P(None, "blk"), P(None, "blk")),
        check_vma=False,
    )
```

```python
import functools

import jax
import jax.numpy as jnp
from jax import lax
from jax.experimental import pallas as pl
from jax.experimental.pallas import tpu as pltpu
from jax.sharding import PartitionSpec as P

W = 8
SLOTS = W // 2
ROWS = 256
SUB = 16
DEPTH = 512
MESH = pl.DeviceIdType.MESH
f32 = jnp.float32
bf16 = jnp.bfloat16


def split3(value):
    hi = value.astype(bf16).astype(f32)
    rest = value - hi
    mid = rest.astype(bf16).astype(f32)
    return hi, mid, rest - mid


def lanes(value):
    total = value[:, 0:128]
    for at in range(128, value.shape[1], 128):
        total = total + value[:, at : at + 128]
    return total


def kernel(
    n, points, scale, noise, target, listed, sol, res,
    z, zp, left, right, sq, tiles, diag, rowacc, total, image, resid, low,
    vp1, vp2, out1, in1, out2, in2, half1, half2, mine, sums,
    acc, outd, ind, zs, zr, ds, dr, v1s, v1r, v2s, v2r, r1s, r1r, r2s, r2r, hs, hr, ss, sr,
):
    blk = lax.axis_index("blk")
    core = lax.axis_index("rep")
    feats, size = points.shape
    cols = target.shape[0]
    half = size // 2

    def offset(k):
        return 1 + 2 * k + core

    def at(block):
        return {"blk": block, "rep": core}

    first = lax.div(blk, 4) * 4

    def mate(m):
        return first + lax.rem(blk - first + m, 4)

    barrier = pltpu.get_barrier_semaphore()

    @pl.loop(0, n)
    def _(b):
        @pl.when(b != blk)
        def _():
            pl.semaphore_signal(barrier, inc=1, device_id=at(b), device_id_type=MESH)

    for m in range(4):
        pl.semaphore_signal(
            barrier, inc=1, device_id={"blk": mate(m), "rep": 1 - core}, device_id_type=MESH
        )
    scaled = points[...] / scale[...]
    z[...] = scaled
    low[0] = target[...].astype(bf16)
    pl.semaphore_wait(barrier, n + 3)

    def copy(src, dst, send, recv, block):
        return pltpu.make_async_remote_copy(
            src_ref=src, dst_ref=dst, send_sem=send, recv_sem=recv,
            device_id=at(block), device_id_type=MESH,
        )

    def z_send(src, shift, block, sem):
        slot, owner = lax.div(shift - 1, 2), lax.rem(shift - 1, 2)
        return pltpu.make_async_remote_copy(
            src_ref=src, dst_ref=zp.at[slot], send_sem=zs.at[sem], recv_sem=zr.at[slot],
            device_id={"blk": block, "rep": owner}, device_id_type=MESH,
        )

    def z_wait(k):
        copy(z, zp.at[k], zs.at[0], zr.at[k], blk).wait_recv()

    def own_sends(act):
        for m in (1, 2, 3):
            @pl.when((core == 0) & (mate(m) < blk))
            def _(m=m):
                act(z_send(z, blk - mate(m), mate(m), m - 1))

        @pl.when((core == 1) & (blk >= 4))
        def _():
            act(z_send(z, 4, blk - 4, 0))

    def relay_near(act):
        @pl.when(blk >= 4)
        def _():
            act(z_send(zp.at[1], 8, blk - 4, 1))

        for m in (1, 2, 3):
            act(z_send(zp.at[1], blk + 4 - mate(m), mate(m), 1 + m))

    def relay_far(act):
        for m in (1, 2, 3):
            @pl.when(mate(m) > blk)
            def _(m=m):
                act(z_send(zp.at[3], blk + 8 - mate(m), mate(m), 4 + m))

    def deg_copy(k):
        return copy(outd.at[k], ind.at[k], ds.at[k], dr.at[k], blk + offset(k))

    def v1_copy(k):
        return copy(low.at[0], vp1.at[k], v1s.at[k], v1r.at[k], blk - offset(k))

    def v2_copy(k):
        return copy(low.at[1], vp2.at[k], v2s.at[k], v2r.at[k], blk - offset(k))

    def ret1_copy(k):
        return copy(out1.at[k], in1.at[k], r1s.at[k], r1r.at[k], blk + offset(k))

    def ret2_copy(k):
        return copy(out2.at[k], in2.at[k], r2s.at[k], r2r.at[k], blk + offset(k))

    def below(k):
        return blk - offset(k) >= 0

    def above(k):
        return blk + offset(k) < n

    own_sends(lambda one: one.start())

    for k in range(SLOTS):
        @pl.when(below(k))
        def _(k=k):
            v1_copy(k).start()

    def norm_rows(value, first):
        n1, n2, n3 = split3(jnp.sum(value * value, axis=0, keepdims=True))
        i = lax.broadcasted_iota(jnp.int32, (16, size), 0)
        ones = jnp.where((i >= 3 - first) & (i < 6 - first), 1.0, 0.0)
        return jnp.where(
            i == first, n1, jnp.where(i == first + 1, n2, jnp.where(i == first + 2, n3, ones))
        )

    def fill_right(value):
        hi, mid, lo = split3(value)
        for j, part in enumerate((hi, mid, hi, mid, lo, hi)):
            right[j * feats : (j + 1) * feats, :] = part.astype(bf16)
        right[6 * feats : 6 * feats + 16, :] = norm_rows(value, 3).astype(bf16)

    right[6 * feats + 16 :, :] = jnp.zeros((DEPTH - 6 * feats - 16, size), bf16)
    hi, mid, lo = split3(-2.0 * scaled)
    hi2 = jnp.concatenate([hi, hi], axis=0)
    mid2 = jnp.concatenate([mid, mid], axis=0)
    hilo = jnp.concatenate([hi, lo], axis=0)
    tail = jnp.concatenate(
        [norm_rows(scaled, 0), jnp.zeros((112, size), f32)], axis=0
    )
    for j, part in enumerate((hi2, mid2, hilo, tail)):
        left[:, j * 128 : (j + 1) * 128] = part.T.astype(bf16)
    fill_right(scaled)

    def chunk(row, store, weight, with_rows, colacc):
        sq[...] = jnp.dot(
            left[pl.ds(row, ROWS), :], right[...], preferred_element_type=f32
        )
        for sub in range(0, ROWS, SUB):
            square = jnp.maximum(sq[sub : sub + SUB, :], 1e-24)
            radius = square * lax.rsqrt(square)
            margin = jnp.maximum(1.0 - radius, 0.0)
            margin = margin * margin
            value = margin * margin * (radius * (4.0 * weight) + weight)
            store(sub, value.astype(bf16))
            for g in range(0, SUB, 8):
                colacc = colacc + value[g : g + 8, :]
            if with_rows:
                rowacc[pl.ds(pl.multiple_of(row + sub, 8), SUB), :] += lanes(value)
        return colacc

    rowacc[...] = jnp.zeros_like(rowacc)
    inv = 1.0 / size

    def diag_chunk(j, colacc):
        def store(sub, value):
            diag[pl.ds(pl.multiple_of(j * ROWS + sub, 16), SUB), :] = value

        row = pl.multiple_of(core * half + j * ROWS, ROWS)
        return chunk(row, store, inv, False, colacc)

    @pl.when((core == 1) & (blk + 4 < n))
    def _():
        z_wait(1)
        relay_near(lambda one: one.start())

    colacc = lax.fori_loop(0, half // ROWS, diag_chunk, jnp.zeros((8, size), f32))
    own_cols = pl.ds(pl.multiple_of(core * half, 128), half)
    total[0:cols, :] = jnp.dot(low[0, :, own_cols], diag[...], preferred_element_type=f32)
    total[cols:, :] = jnp.zeros((8, size), f32)
    total[cols : cols + 1, :] = jnp.sum(colacc, axis=0, keepdims=True)

    acc[...] = jnp.zeros_like(acc)

    def back(value, tile):
        wide = jnp.concatenate(
            [value.astype(f32), jnp.zeros((128 - cols, size), f32)], axis=0
        )
        acc[...] += jnp.dot(tile, wide.T.astype(bf16), preferred_element_type=f32)

    @pl.when((core == 1) & (blk + 8 < n))
    def _():
        z_wait(3)
        relay_far(lambda one: one.start())

    @pl.loop(0, SLOTS)
    def _(step_k):
        k = lax.rem(step_k + core, SLOTS)

        @pl.when(above(k))
        def _():
            @pl.when((core == 0) | (lax.rem(k, 2) == 0))
            def _():
                z_wait(k)

            v1_copy(k).wait_recv()
            fill_right(zp[k])
            weight = listed[0, offset(k) - 1] * inv

            def step(j, colacc):
                def store(sub, value):
                    tiles[k, pl.ds(pl.multiple_of(j * ROWS + sub, 16), SUB), :] = value

                return chunk(pl.multiple_of(j * ROWS, ROWS), store, weight, True, colacc)

            colacc = lax.fori_loop(0, size // ROWS, step, jnp.zeros((8, size), f32))
            tile = tiles.at[k]
            outd[k] = jnp.sum(colacc, axis=0, keepdims=True)
            deg_copy(k).start()
            out1[k] = jnp.dot(low[0], tile[...], preferred_element_type=f32)
            ret1_copy(k).start()
            back(vp1[k], tile[...])

    total[0:cols, :] += acc[...].T[0:cols, :]
    acc[...] = jnp.zeros_like(acc)
    total[cols : cols + 1, :] += jnp.sum(rowacc[...].T, axis=0, keepdims=True)

    def collect(inbox, get, dst, send, recv):
        for k in range(SLOTS):
            @pl.when(below(k))
            def _(k=k):
                get(k).wait_recv()
                total[0:cols, :] += inbox[k]

        src = total.at[pl.ds(0, dst.shape[0])]
        swap = pltpu.make_async_remote_copy(
            src_ref=src, dst_ref=dst, send_sem=send, recv_sem=recv,
            device_id={"blk": blk, "rep": 1 - core}, device_id_type=MESH,
        )
        swap.start()
        swap.wait()

    def spot(j):
        row = lax.broadcasted_iota(jnp.int32, (cols, 128), 0)
        return lax.broadcasted_iota(jnp.int32, (cols, 128), 1) == row + j * cols

    def sum_start(which, values):
        mine[which] = sum(
            jnp.sum(
                jnp.where(spot(j), jnp.sum(value, axis=1, keepdims=True), 0.0),
                axis=0, keepdims=True,
            )
            for j, value in enumerate(values)
        )
        sums[which, pl.ds(blk, 1)] = mine[pl.ds(which, 1)]

        @pl.loop(0, n)
        def _(b):
            @pl.when(b != blk)
            def _():
                copy(mine.at[which], sums.at[which, blk], ss.at[which, b], sr.at[which, blk], b).start()

    def sum_end(which, count):
        @pl.loop(0, n)
        def _(b):
            @pl.when(b != blk)
            def _():
                one = copy(mine.at[which], sums.at[which, b], ss.at[which, b], sr.at[which, b], b)
                one.wait_recv()
                one.wait_send()

        row = jnp.sum(sums[which], axis=0)
        return [
            jnp.sum(jnp.where(spot(j), row, 0.0), axis=1, keepdims=True) for j in range(count)
        ]

    for k in range(SLOTS):
        @pl.when(below(k))
        def _(k=k):
            deg_copy(k).wait_recv()
            total[cols : cols + 1, :] += ind[k]

    collect(in1, ret1_copy, half1, hs.at[0], hr.at[0])
    total[...] += half1[...]
    direction = target[...]
    diagonal = total[cols : cols + 1, :] + noise[...]
    image[...] = diagonal * direction + total[0:cols, :]
    sum_start(0, (direction * direction, direction * image[...]))
    norm_now, curve = sum_end(0, 2)
    step1 = norm_now / curve
    residual = target[...] - step1 * image[...]
    resid[...] = residual
    low[1] = residual.astype(bf16)
    for k in range(SLOTS):
        @pl.when(below(k))
        def _(k=k):
            v2_copy(k).start()
    sum_start(1, (residual * residual,))

    total[0:cols, :] = jnp.dot(low[1, :, own_cols], diag[...], preferred_element_type=f32)

    @pl.loop(0, SLOTS)
    def _(k):
        @pl.when(above(k))
        def _():
            out2[k] = jnp.dot(low[1], tiles[k], preferred_element_type=f32)
            ret2_copy(k).start()

    @pl.loop(0, SLOTS)
    def _(k):
        @pl.when(above(k))
        def _():
            v2_copy(k).wait_recv()
            back(vp2[k], tiles[k])

    total[0:cols, :] += acc[...].T[0:cols, :]

    norm_next = sum_end(1, 1)[0]
    collect(in2, ret2_copy, half2, hs.at[1], hr.at[1])
    beta = norm_next / norm_now
    direction = resid[...] + beta * target[...]
    image2 = (
        diagonal * resid[...] + (total[0:cols, :] + half2[...]) + beta * image[...]
    )
    sum_start(2, (direction * image2,))
    step2 = norm_next / sum_end(2, 1)[0]
    sol[...] = step1 * target[...] + step2 * direction
    res[...] = resid[...] - step2 * image2

    own_sends(lambda one: one.wait_send())

    @pl.when((core == 1) & (blk + 4 < n))
    def _():
        relay_near(lambda one: one.wait_send())

    @pl.when((core == 1) & (blk + 8 < n))
    def _():
        relay_far(lambda one: one.wait_send())

    for k in range(SLOTS):
        @pl.when(below(k))
        def _(k=k):
            v1_copy(k).wait_send()
            v2_copy(k).wait_send()

        @pl.when(above(k))
        def _(k=k):
            ret1_copy(k).wait_send()
            deg_copy(k).wait_send()
            ret2_copy(k).wait_send()


def body(n, points, lengthscale, noise, target, pair_offset, pair_count):
    feats, size = points.shape
    cols = target.shape[0]
    live = jnp.arange(W)[None, :] < pair_count[:, None]
    match = pair_offset[0][None, :] == jnp.arange(1, W + 1)[:, None]
    listed = jnp.any(match & live, axis=1).astype(f32)[None, :]
    vmem = pl.BlockSpec(memory_space=pltpu.VMEM)
    dma = pltpu.SemaphoreType.DMA
    V = pltpu.VMEM
    return pl.pallas_call(
        functools.partial(kernel, n),
        out_shape=[jax.ShapeDtypeStruct((cols, size), f32)] * 2,
        in_specs=[vmem, vmem, vmem, vmem, pl.BlockSpec(memory_space=pltpu.SMEM)],
        out_specs=[vmem, vmem],
        scratch_shapes=[
            V((feats, size), f32),
            V((SLOTS, feats, size), f32),
            V((size, DEPTH), bf16),
            V((DEPTH, size), bf16),
            V((ROWS, size), f32),
            V((SLOTS, size, size), bf16),
            V((size // 2, size), bf16),
            V((size, 128), f32),
            V((cols + 8, size), f32),
            V((cols, size), f32),
            V((cols, size), f32),
            V((2, cols, size), bf16),
            V((SLOTS, cols, size), bf16),
            V((SLOTS, cols, size), bf16),
            V((SLOTS, cols, size), f32),
            V((SLOTS, cols, size), f32),
            V((SLOTS, cols, size), f32),
            V((SLOTS, cols, size), f32),
            V((cols + 8, size), f32),
            V((cols, size), f32),
            V((3, 1, 128), f32),
            V((3, n, 1, 128), f32),
            V((size, 128), f32),
            V((SLOTS, 1, size), f32),
            V((SLOTS, 1, size), f32),
        ]
        + [dma((W,)), dma((SLOTS,))]
        + [dma((SLOTS,))] * 10
        + [dma((2,))] * 2
        + [dma((3, n))] * 2,
        compiler_params=pltpu.CompilerParams(
            collective_id=0, has_side_effects=True, vmem_limit_bytes=48 * 1024 * 1024
        ),
    )(points, lengthscale[:, None], noise[None, :], target, listed)


def solution(mesh):
    n = mesh.shape["blk"]
    placed = (P(None, "blk"), P(), P("blk"), P(None, "blk"), P("blk", None), P("blk"))
    return jax.shard_map(
        functools.partial(body, n),
        mesh=mesh,
        in_specs=placed,
        out_specs=(P(None, "blk"), P(None, "blk")),
        check_vma=False,
    )
```

```python
import functools

import jax
import jax.numpy as jnp
from jax import lax
from jax.experimental import pallas as pl
from jax.experimental.pallas import tpu as pltpu
from jax.sharding import PartitionSpec as P

W = 8
SLOTS = W // 2
ROWS = 256
SUB = 16
DEPTH = 512
MESH = pl.DeviceIdType.MESH
f32 = jnp.float32
bf16 = jnp.bfloat16


def split3(value):
    hi = value.astype(bf16).astype(f32)
    rest = value - hi
    mid = rest.astype(bf16).astype(f32)
    return hi, mid, rest - mid


def lanes(value):
    total = value[:, 0:128]
    for at in range(128, value.shape[1], 128):
        total = total + value[:, at : at + 128]
    return total


def kernel(
    n, points_hbm, scale_hbm, noise_hbm, target_hbm, offsets, count, sol, res,
    points, scale, noise, target, loads,
    z, zp, left, right, sq, tiles, diag, rowacc, total, image, resid, low,
    vp1, vp2, out1, in1, out2, in2, half1, half2, mine, sums,
    acc, outd, ind, zs, zr, ds, dr, v1s, v1r, v2s, v2r, r1s, r1r, r2s, r2r, hs, hr, ss, sr,
):
    blk = lax.axis_index("blk")
    core = lax.axis_index("rep")
    feats, size = points.shape
    cols = target.shape[0]
    half = size // 2

    def offset(k):
        return 1 + 2 * k + core

    def at(block):
        return {"blk": block, "rep": core}

    first = lax.div(blk, 4) * 4

    def mate(m):
        return first + lax.rem(blk - first + m, 4)

    fetches = [
        pltpu.make_async_copy(src, dst, loads.at[j])
        for j, (src, dst) in enumerate(
            ((points_hbm, points), (scale_hbm, scale), (target_hbm, target), (noise_hbm, noise))
        )
    ]
    for fetch in fetches:
        fetch.start()

    barrier = pltpu.get_barrier_semaphore()

    @pl.loop(0, n)
    def _(b):
        @pl.when(b != blk)
        def _():
            pl.semaphore_signal(barrier, inc=1, device_id=at(b), device_id_type=MESH)

    for m in range(4):
        pl.semaphore_signal(
            barrier, inc=1, device_id={"blk": mate(m), "rep": 1 - core}, device_id_type=MESH
        )
    for fetch in fetches:
        fetch.wait()
    scaled = points[...] / scale[...]
    z[...] = scaled
    low[0] = target[...].astype(bf16)
    pl.semaphore_wait(barrier, n + 3)

    def copy(src, dst, send, recv, block):
        return pltpu.make_async_remote_copy(
            src_ref=src, dst_ref=dst, send_sem=send, recv_sem=recv,
            device_id=at(block), device_id_type=MESH,
        )

    def z_send(src, shift, block, sem):
        slot, owner = lax.div(shift - 1, 2), lax.rem(shift - 1, 2)
        return pltpu.make_async_remote_copy(
            src_ref=src, dst_ref=zp.at[slot], send_sem=zs.at[sem], recv_sem=zr.at[slot],
            device_id={"blk": block, "rep": owner}, device_id_type=MESH,
        )

    def z_wait(k):
        copy(z, zp.at[k], zs.at[0], zr.at[k], blk).wait_recv()

    def own_sends(act):
        for m in (1, 2, 3):
            @pl.when((core == 0) & (mate(m) < blk))
            def _(m=m):
                act(z_send(z, blk - mate(m), mate(m), m - 1))

        @pl.when((core == 1) & (blk >= 4))
        def _():
            act(z_send(z, 4, blk - 4, 0))

    def relay_near(act):
        @pl.when(blk >= 4)
        def _():
            act(z_send(zp.at[1], 8, blk - 4, 1))

        for m in (1, 2, 3):
            act(z_send(zp.at[1], blk + 4 - mate(m), mate(m), 1 + m))

    def relay_far(act):
        for m in (1, 2, 3):
            @pl.when(mate(m) > blk)
            def _(m=m):
                act(z_send(zp.at[3], blk + 8 - mate(m), mate(m), 4 + m))

    def deg_copy(k):
        return copy(outd.at[k], ind.at[k], ds.at[k], dr.at[k], blk + offset(k))

    def v1_copy(k):
        return copy(low.at[0], vp1.at[k], v1s.at[k], v1r.at[k], blk - offset(k))

    def v2_copy(k):
        return copy(low.at[1], vp2.at[k], v2s.at[k], v2r.at[k], blk - offset(k))

    def ret1_copy(k):
        return copy(out1.at[k], in1.at[k], r1s.at[k], r1r.at[k], blk + offset(k))

    def ret2_copy(k):
        return copy(out2.at[k], in2.at[k], r2s.at[k], r2r.at[k], blk + offset(k))

    def below(k):
        return blk - offset(k) >= 0

    def above(k):
        return blk + offset(k) < n

    own_sends(lambda one: one.start())

    for k in range(SLOTS):
        @pl.when(below(k))
        def _(k=k):
            v1_copy(k).start()

    def norm_rows(value, first):
        n1, n2, n3 = split3(jnp.sum(value * value, axis=0, keepdims=True))
        i = lax.broadcasted_iota(jnp.int32, (16, size), 0)
        ones = jnp.where((i >= 3 - first) & (i < 6 - first), 1.0, 0.0)
        return jnp.where(
            i == first, n1, jnp.where(i == first + 1, n2, jnp.where(i == first + 2, n3, ones))
        )

    def fill_right(value):
        hi, mid, lo = split3(value)
        for j, part in enumerate((hi, mid, hi, mid, lo, hi)):
            right[j * feats : (j + 1) * feats, :] = part.astype(bf16)
        right[6 * feats : 6 * feats + 16, :] = norm_rows(value, 3).astype(bf16)

    right[6 * feats + 16 :, :] = jnp.zeros((DEPTH - 6 * feats - 16, size), bf16)
    hi, mid, lo = split3(-2.0 * scaled)
    hi2 = jnp.concatenate([hi, hi], axis=0)
    mid2 = jnp.concatenate([mid, mid], axis=0)
    hilo = jnp.concatenate([hi, lo], axis=0)
    tail = jnp.concatenate(
        [norm_rows(scaled, 0), jnp.zeros((112, size), f32)], axis=0
    )
    for j, part in enumerate((hi2, mid2, hilo, tail)):
        left[:, j * 128 : (j + 1) * 128] = part.T.astype(bf16)
    fill_right(scaled)

    def chunk(row, store, weight, with_rows, colacc):
        sq[...] = jnp.dot(
            left[pl.ds(row, ROWS), :], right[...], preferred_element_type=f32
        )
        for sub in range(0, ROWS, SUB):
            square = jnp.maximum(sq[sub : sub + SUB, :], 1e-24)
            radius = square * lax.rsqrt(square)
            margin = jnp.maximum(1.0 - radius, 0.0)
            margin = margin * margin
            value = margin * margin * (radius * (4.0 * weight) + weight)
            store(sub, value.astype(bf16))
            for g in range(0, SUB, 8):
                colacc = colacc + value[g : g + 8, :]
            if with_rows:
                rowacc[pl.ds(pl.multiple_of(row + sub, 8), SUB), :] += lanes(value)
        return colacc

    rowacc[...] = jnp.zeros_like(rowacc)
    inv = 1.0 / size

    def diag_chunk(j, colacc):
        def store(sub, value):
            diag[pl.ds(pl.multiple_of(j * ROWS + sub, 16), SUB), :] = value

        row = pl.multiple_of(core * half + j * ROWS, ROWS)
        return chunk(row, store, inv, False, colacc)

    @pl.when((core == 1) & (blk + 4 < n))
    def _():
        z_wait(1)
        relay_near(lambda one: one.start())

    colacc = lax.fori_loop(0, half // ROWS, diag_chunk, jnp.zeros((8, size), f32))
    own_cols = pl.ds(pl.multiple_of(core * half, 128), half)
    total[0:cols, :] = jnp.dot(low[0, :, own_cols], diag[...], preferred_element_type=f32)
    total[cols:, :] = jnp.zeros((8, size), f32)
    total[cols : cols + 1, :] = jnp.sum(colacc, axis=0, keepdims=True)

    acc[...] = jnp.zeros_like(acc)

    def back(value, tile):
        wide = jnp.concatenate(
            [value.astype(f32), jnp.zeros((128 - cols, size), f32)], axis=0
        )
        acc[...] += jnp.dot(tile, wide.T.astype(bf16), preferred_element_type=f32)

    @pl.when((core == 1) & (blk + 8 < n))
    def _():
        z_wait(3)
        relay_far(lambda one: one.start())

    @pl.loop(0, SLOTS)
    def _(step_k):
        k = lax.rem(step_k + core, SLOTS)

        @pl.when(above(k))
        def _():
            @pl.when((core == 0) | (lax.rem(k, 2) == 0))
            def _():
                z_wait(k)

            v1_copy(k).wait_recv()
            fill_right(zp[k])
            weight = sum(
                jnp.where((offsets[0, s] == offset(k)) & (s < count[0]), inv, 0.0)
                for s in range(W)
            )

            def step(j, colacc):
                def store(sub, value):
                    tiles[k, pl.ds(pl.multiple_of(j * ROWS + sub, 16), SUB), :] = value

                return chunk(pl.multiple_of(j * ROWS, ROWS), store, weight, True, colacc)

            colacc = lax.fori_loop(0, size // ROWS, step, jnp.zeros((8, size), f32))
            tile = tiles.at[k]
            outd[k] = jnp.sum(colacc, axis=0, keepdims=True)
            deg_copy(k).start()
            out1[k] = jnp.dot(low[0], tile[...], preferred_element_type=f32)
            ret1_copy(k).start()
            back(vp1[k], tile[...])

    total[0:cols, :] += acc[...].T[0:cols, :]
    acc[...] = jnp.zeros_like(acc)
    total[cols : cols + 1, :] += jnp.sum(rowacc[...].T, axis=0, keepdims=True)

    def collect(inbox, get, dst, send, recv):
        for k in range(SLOTS):
            @pl.when(below(k))
            def _(k=k):
                get(k).wait_recv()
                total[0:cols, :] += inbox[k]

        src = total.at[pl.ds(0, dst.shape[0])]
        swap = pltpu.make_async_remote_copy(
            src_ref=src, dst_ref=dst, send_sem=send, recv_sem=recv,
            device_id={"blk": blk, "rep": 1 - core}, device_id_type=MESH,
        )
        swap.start()
        swap.wait()

    def spot(j):
        row = lax.broadcasted_iota(jnp.int32, (cols, 128), 0)
        return lax.broadcasted_iota(jnp.int32, (cols, 128), 1) == row + j * cols

    def sum_start(which, values):
        mine[which] = sum(
            jnp.sum(
                jnp.where(spot(j), jnp.sum(value, axis=1, keepdims=True), 0.0),
                axis=0, keepdims=True,
            )
            for j, value in enumerate(values)
        )
        sums[which, pl.ds(blk, 1)] = mine[pl.ds(which, 1)]

        @pl.loop(0, n)
        def _(b):
            @pl.when(b != blk)
            def _():
                copy(mine.at[which], sums.at[which, blk], ss.at[which, b], sr.at[which, blk], b).start()

    def sum_end(which, count):
        @pl.loop(0, n)
        def _(b):
            @pl.when(b != blk)
            def _():
                one = copy(mine.at[which], sums.at[which, b], ss.at[which, b], sr.at[which, b], b)
                one.wait_recv()
                one.wait_send()

        row = jnp.sum(sums[which], axis=0)
        return [
            jnp.sum(jnp.where(spot(j), row, 0.0), axis=1, keepdims=True) for j in range(count)
        ]

    for k in range(SLOTS):
        @pl.when(below(k))
        def _(k=k):
            deg_copy(k).wait_recv()
            total[cols : cols + 1, :] += ind[k]

    collect(in1, ret1_copy, half1, hs.at[0], hr.at[0])
    total[...] += half1[...]
    direction = target[...]
    diagonal = total[cols : cols + 1, :] + noise[...]
    image[...] = diagonal * direction + total[0:cols, :]
    sum_start(0, (direction * direction, direction * image[...]))
    norm_now, curve = sum_end(0, 2)
    step1 = norm_now / curve
    residual = target[...] - step1 * image[...]
    resid[...] = residual
    low[1] = residual.astype(bf16)
    for k in range(SLOTS):
        @pl.when(below(k))
        def _(k=k):
            v2_copy(k).start()
    sum_start(1, (residual * residual,))

    total[0:cols, :] = jnp.dot(low[1, :, own_cols], diag[...], preferred_element_type=f32)

    @pl.loop(0, SLOTS)
    def _(k):
        @pl.when(above(k))
        def _():
            out2[k] = jnp.dot(low[1], tiles[k], preferred_element_type=f32)
            ret2_copy(k).start()

    @pl.loop(0, SLOTS)
    def _(k):
        @pl.when(above(k))
        def _():
            v2_copy(k).wait_recv()
            back(vp2[k], tiles[k])

    total[0:cols, :] += acc[...].T[0:cols, :]

    norm_next = sum_end(1, 1)[0]
    collect(in2, ret2_copy, half2, hs.at[1], hr.at[1])
    beta = norm_next / norm_now
    direction = resid[...] + beta * target[...]
    image2 = (
        diagonal * resid[...] + (total[0:cols, :] + half2[...]) + beta * image[...]
    )
    sum_start(2, (direction * image2,))
    step2 = norm_next / sum_end(2, 1)[0]
    sol[...] = step1 * target[...] + step2 * direction
    res[...] = resid[...] - step2 * image2

    own_sends(lambda one: one.wait_send())

    @pl.when((core == 1) & (blk + 4 < n))
    def _():
        relay_near(lambda one: one.wait_send())

    @pl.when((core == 1) & (blk + 8 < n))
    def _():
        relay_far(lambda one: one.wait_send())

    for k in range(SLOTS):
        @pl.when(below(k))
        def _(k=k):
            v1_copy(k).wait_send()
            v2_copy(k).wait_send()

        @pl.when(above(k))
        def _(k=k):
            ret1_copy(k).wait_send()
            deg_copy(k).wait_send()
            ret2_copy(k).wait_send()


def body(n, points, lengthscale, noise, target, pair_offset, pair_count):
    feats, size = points.shape
    cols = target.shape[0]
    vmem = pl.BlockSpec(memory_space=pltpu.VMEM)
    dma = pltpu.SemaphoreType.DMA
    V = pltpu.VMEM
    return pl.pallas_call(
        functools.partial(kernel, n),
        out_shape=[jax.ShapeDtypeStruct((cols, size), f32)] * 2,
        in_specs=[pl.BlockSpec(memory_space=pltpu.HBM)] * 4
        + [pl.BlockSpec(memory_space=pltpu.SMEM)] * 2,
        out_specs=[vmem, vmem],
        scratch_shapes=[
            V((feats, size), f32),
            V((feats, 1), f32),
            V((1, size), f32),
            V((cols, size), f32),
            dma((4,)),
            V((feats, size), f32),
            V((SLOTS, feats, size), f32),
            V((size, DEPTH), bf16),
            V((DEPTH, size), bf16),
            V((ROWS, size), f32),
            V((SLOTS, size, size), bf16),
            V((size // 2, size), bf16),
            V((size, 128), f32),
            V((cols + 8, size), f32),
            V((cols, size), f32),
            V((cols, size), f32),
            V((2, cols, size), bf16),
            V((SLOTS, cols, size), bf16),
            V((SLOTS, cols, size), bf16),
            V((SLOTS, cols, size), f32),
            V((SLOTS, cols, size), f32),
            V((SLOTS, cols, size), f32),
            V((SLOTS, cols, size), f32),
            V((cols + 8, size), f32),
            V((cols, size), f32),
            V((3, 1, 128), f32),
            V((3, n, 1, 128), f32),
            V((size, 128), f32),
            V((SLOTS, 1, size), f32),
            V((SLOTS, 1, size), f32),
        ]
        + [dma((W,)), dma((SLOTS,))]
        + [dma((SLOTS,))] * 10
        + [dma((2,))] * 2
        + [dma((3, n))] * 2,
        compiler_params=pltpu.CompilerParams(
            collective_id=0, has_side_effects=True, vmem_limit_bytes=63 * 1024 * 1024
        ),
    )(points, lengthscale[:, None], noise[None, :], target, pair_offset, pair_count)


def solution(mesh):
    n = mesh.shape["blk"]
    placed = (P(None, "blk"), P(), P("blk"), P(None, "blk"), P("blk", None), P("blk"))
    return jax.shard_map(
        functools.partial(body, n),
        mesh=mesh,
        in_specs=placed,
        out_specs=(P(None, "blk"), P(None, "blk")),
        check_vma=False,
    )
```
